256 devices in a mesh: row: 16 (over z_lo, x, core), col: 16 (over z_hi, y).
Axes of the slice: x: 4, y: 4, z: 8 (z_hi: 4, z_lo: 2; z = z_hi * 2 + z_lo), core: 2. Of those that a mesh axis runs over, the one named last changes fastest.
Arguments:
- tokens: bfloat16 [2048, 6144], P('row', 'col'), may hold values from -6 to 6
- out_grad: bfloat16 [2048, 6144], P('row', 'col'), may hold values from -6 to 6
- pre_act: bfloat16 [2048, 24576], P('col', 'row'), may hold values from -6 to 6
- w_in: bfloat16 [6144, 24576], P('col', 'row'), may hold values from -0.078125 to 0.078125
- w_out: bfloat16 [24576, 6144], P('row', 'col'), may hold values from -0.0390625 to 0.0390625
Outputs:
- grad_tokens: bfloat16 [2048, 6144], P('row', 'col')
- grad_w_in: bfloat16 [6144, 24576], P('col', 'row')
- grad_w_out: bfloat16 [24576, 6144], P('row', 'col')
The draws below stay inside these ranges and needn't reach their ends.
All inputs are finite; a program needn't handle non-finite values.
Results may differ from the reference program's by a relative error of at most 0.03.
Values may be sent and summed in bfloat16 or wider, within the bound.
No kernel may reach another device: no remote copies, remote signals or barrier semaphores. Data moves between devices by JAX's collectives and lax.ppermute only.
A program may use at most 128 MiB of HBM per device.

```python
import math
import jax
import jax.numpy as jnp
from jax import lax

D = 6144
FF = 24576
TOKENS = 2048
N_ROW = 16
N_COL = 16


def levels(rng, shape, shards, low, high):
    def one(position, parts):
        draws = jax.random.uniform(jax.random.fold_in(jax.random.fold_in(rng, 6), position), (parts,), jnp.float32, low / len(shards), high / len(shards))
        return jnp.repeat(jnp.exp(draws), shape[position] // parts).reshape((-1,) + (1,) * (len(shape) - position - 1))

    gain = one(*shards[0])
    for cut in shards[1:]:
        gain = gain * one(*cut)
    return gain


def scatter_about(rng, shape, deviation, limit, pieces=(), dtype=jnp.bfloat16):
    loudness = levels(rng, shape, pieces, -0.22, 0.18) if pieces else 1.0
    result = jax.random.normal(rng, shape, jnp.float32) * deviation * loudness
    return jnp.minimum(jnp.maximum(result, -limit), limit).astype(dtype)


def setup_inputs(seed: int = 0) -> dict:
    keys = jax.random.split(jax.random.key(seed), 6)
    return {
        "tokens": scatter_about(keys[0], (TOKENS, D), 1.0, 6.0, ((0, 16), (1, 16))),
        "out_grad": scatter_about(keys[1], (TOKENS, D), 1.0, 6.0, ((0, 16), (1, 16))),
        "pre_act": scatter_about(keys[2], (TOKENS, FF), 1.5, 6.0, ((0, 16), (1, 16))),
        "w_in": scatter_about(keys[3], (D, FF), D ** -0.5, 0.078125, ((0, 16), (1, 16))),
        "w_out": scatter_about(keys[4], (FF, D), FF ** -0.5, 0.0390625, ((0, 16), (1, 16))),
    }


gelu_coef = math.sqrt(2.0 / math.pi)
cubic_coef = 0.044715

def gelu_parts(pre_values):
    pre_f32 = pre_values.astype(jnp.float32)
    tangent = jnp.tanh(gelu_coef * (pre_f32 + cubic_coef * pre_f32 * pre_f32 * pre_f32))
    activated = 0.5 * pre_f32 * (1.0 + tangent)
    slopes = 0.5 * (1.0 + tangent) + 0.5 * pre_f32 * (1.0 - tangent * tangent) * gelu_coef * (1.0 + 3.0 * cubic_coef * pre_f32 * pre_f32)
    return (activated, slopes)

def contract(left_side, right_side, left_dim, right_dim):
    return lax.dot_general(left_side, right_side, (((left_dim,), (right_dim,)), ((), ())), preferred_element_type=jnp.float32)

def reference(tokens, out_grad, pre_act, w_in, w_out):
    activated, slopes = gelu_parts(pre_act)
    hidden = activated.astype(jnp.bfloat16)
    block_width = D // N_COL
    hidden_grad = jnp.zeros((TOKENS, FF), jnp.float32)
    for block in range(N_COL):
        lower = block * block_width
        partial_term = contract(out_grad[:, lower:lower + block_width], w_out[:, lower:lower + block_width], 1, 1)
        rounded = lax.optimization_barrier(partial_term.astype(jnp.bfloat16))
        hidden_grad = hidden_grad + rounded.astype(jnp.float32)
    pre_grad = (hidden_grad * slopes).astype(jnp.bfloat16)
    grad_scale = float(TOKENS) ** (-0.5)
    grad_w_out = (contract(hidden, out_grad, 0, 0) * grad_scale).astype(jnp.bfloat16)
    grad_w_in = (contract(tokens, pre_grad, 0, 0) * grad_scale).astype(jnp.bfloat16)
    unit_width = FF // N_ROW
    token_total = jnp.zeros((TOKENS, D), jnp.float32)
    for block in range(N_ROW):
        lower = block * unit_width
        partial_term = contract(pre_grad[:, lower:lower + unit_width], w_in[:, lower:lower + unit_width], 1, 1)
        rounded = lax.optimization_barrier(partial_term.astype(jnp.bfloat16))
        token_total = token_total + rounded.astype(jnp.float32)
    grad_tokens = token_total.astype(jnp.bfloat16)
    return (grad_tokens, grad_w_in, grad_w_out)
```

```python
import math

import jax
import jax.numpy as jnp
from jax import lax
from jax.experimental import pallas as pl
from jax.experimental.pallas import tpu as pltpu
from jax.sharding import Mesh
from jax.sharding import PartitionSpec as P

gelu_coef = math.sqrt(2.0 / math.pi)
cubic_coef = 0.044715
ROW = ("zl", "x", "c")
COL = ("zh", "y")
SIZES = {"zl": 2, "x": 4, "c": 2, "zh": 4, "y": 4}
CHUNKS = 2
ROWS = 128 // CHUNKS
HALF = 768


def gelu_parts(pre_values):
    pre_f32 = pre_values.astype(jnp.float32)
    tangent = jnp.tanh(gelu_coef * (pre_f32 + cubic_coef * pre_f32 * pre_f32 * pre_f32))
    activated = 0.5 * pre_f32 * (1.0 + tangent)
    slopes = 0.5 * (1.0 + tangent) + 0.5 * pre_f32 * (1.0 - tangent * tangent) * gelu_coef * (
        1.0 + 3.0 * cubic_coef * pre_f32 * pre_f32
    )
    return (activated, slopes)


def contract(left_side, right_side, left_dim, right_dim):
    return lax.dot_general(
        left_side,
        right_side,
        (((left_dim,), (right_dim,)), ((), ())),
        preferred_element_type=jnp.float32,
    )


def shift(values, axis, step):
    size = SIZES[axis]
    return lax.ppermute(values, axis, [(i, (i + step) % size) for i in range(size)])


def fence(*values):
    return lax.optimization_barrier(values)


def place_blocks(index_ref, *refs):
    count = sum(1 for ref in refs if len(ref.shape) == 3)
    seen = 0
    for source in refs[:count]:
        for k in range(source.shape[0]):
            for t, target in enumerate(refs[count:]):
                pieces, _, rows, _ = target.shape
                for piece in range(pieces):
                    target[piece, index_ref[t, seen + k]] = source[k, piece * rows : (piece + 1) * rows]
        seen += source.shape[0]


def reorder(index, sources, pieces):
    rows = sources[0].shape[1]
    shapes = [jax.ShapeDtypeStruct((p, 16, rows // p, 384), jnp.bfloat16) for p in pieces]
    moved = 2 * 16 * rows * 384 * (1 + len(pieces))
    return pl.pallas_call(
        place_blocks,
        in_specs=[pl.BlockSpec(memory_space=pltpu.SMEM)]
        + [pl.BlockSpec(memory_space=pltpu.VMEM)] * len(sources),
        out_specs=[pl.BlockSpec(memory_space=pltpu.VMEM)] * len(pieces),
        out_shape=shapes,
        compiler_params=pltpu.CompilerParams(vmem_limit_bytes=16 * 2**20),
        cost_estimate=pl.CostEstimate(flops=0, bytes_accessed=moved, transcendentals=0),
    )(jnp.stack(index), *sources)


def places():
    zl, x, c, zh, y = (lax.axis_index(n) for n in ROW + COL)
    number, wanted = [], []
    for dc in range(2):
        for dzl in range(2):
            for dx in range(4):
                block = ((zl + dzl) % 2 * 4 + (x + dx) % 4) * 2 + (c + dc) % 2
                number.append(block)
                wanted.append((block % 4 - y) % 4 * 4 + (block // 4 - zh) % 4)
    back = [None] * 16
    to_col = []
    for block in range(16):
        to_col.append((block % 4 - y) % 4 * 4 + (block // 4 - zh) % 4)
    for dy in range(4):
        for dz in range(4):
            block = (zh + dz) % 4 * 4 + (y + dy) % 4
            dzl, dx, dc = (block // 8 - zl) % 2, (block // 2 % 4 - x) % 4, (block % 2 - c) % 2
            back[dy * 4 + dz] = (dc * 2 + dzl) * 4 + dx
    return [jnp.stack(i).astype(jnp.int32) for i in (number, wanted, to_col, back)]


def body(tokens, out_grad, pre_act, w_in, w_out):
    number, wanted, to_col, back = places()
    bf16 = jnp.bfloat16
    f32 = jnp.float32
    columns = (slice(0, HALF), slice(HALF, 2 * HALF))

    other = shift(out_grad, "zl", 1)
    activated, slopes = gelu_parts(pre_act)
    act_all = lax.all_gather(activated.astype(bf16), COL, axis=0, tiled=True)
    tok_all = lax.all_gather(tokens, ROW, axis=0, tiled=True).reshape(16, 128, 384)
    pair = jnp.stack([out_grad, other])
    near = [pair, shift(pair, "x", -1), shift(pair, "x", 2), shift(pair, "x", 1)]
    chip = jnp.stack(near, axis=1).reshape(8, 128, 384)
    grad_rel, grad_rows = reorder((wanted, number), (chip, shift(chip, "c", 1)), (CHUNKS, 1))
    grad_rel = grad_rel.reshape(CHUNKS, 4, 4 * ROWS, 384)

    def term(chunk, side, dy):
        return contract(grad_rel[chunk, dy], w_out[columns[side]], 1, 1)

    def scatter_y(chunk, meanwhile):
        sums = (term(chunk, 0, 3).astype(bf16), term(chunk, 1, 1).astype(bf16))
        for hop in (2, 3, 4):
            came = fence(shift(sums[0], "y", 1), shift(sums[1], "y", -1))
            sums = (
                (term(chunk, 0, -hop % 4) + came[0].astype(f32)).astype(bf16),
                (term(chunk, 1, hop % 4) + came[1].astype(f32)).astype(bf16),
            )
        return jnp.concatenate(sums, axis=1).reshape(4, ROWS, 2 * HALF)

    def scatter_z(chunk, sums):
        total = sums[0].astype(f32)
        for dz in (1, 2, 3):
            total = total + shift(sums[dz], "zh", dz).astype(f32)
        return (total * slopes[chunk * ROWS : (chunk + 1) * ROWS]).astype(bf16)

    def gather_z(own):
        return jnp.concatenate([own] + [shift(own, "zh", -dz) for dz in (1, 2, 3)])

    def gather_y(near):
        found = [{0: near[:, columns[0]]}, {0: near[:, columns[1]]}]
        now = (found[0][0], found[1][0])
        for hop in (1, 2, 3):
            now = fence(shift(now[0], "y", 1), shift(now[1], "y", -1))
            found[0][-hop % 4], found[1][hop] = now
        return [jnp.concatenate([found[0][dy], found[1][dy]], axis=1) for dy in range(4)]

    def row_scatter(blocks):
        mine = blocks[:8].astype(f32) + shift(blocks[8:], "c", 1).astype(f32)
        mine = mine.astype(bf16).reshape(2, 4, ROWS, 384)
        total = mine[:, 0].astype(f32)
        for dx in (1, 2, 3):
            total = total + shift(mine[:, dx], "x", dx).astype(f32)
        return total[0] + shift(total[1].astype(bf16), "zl", 1).astype(f32)

    pregrad = [scatter_z(chunk, scatter_y(chunk, None)) for chunk in range(CHUNKS)]
    token_parts, pregrad_all = [], []
    for chunk in range(CHUNKS):
        rows = gather_y(gather_z(pregrad[chunk]))
        parts = [contract(r, w_in, 1, 1).astype(bf16) for r in rows]
        parts = jnp.stack(parts).reshape(16, ROWS, 384)
        (parts,) = reorder((back,), (parts,), (1,))
        token_parts.append(row_scatter(parts[0]).astype(bf16))
        pregrad_all += rows
    grad_tokens = jnp.concatenate(token_parts)
    grad_scale = float(2048) ** (-0.5)
    grad_w_out = (contract(act_all, grad_rows.reshape(2048, 384), 0, 0) * grad_scale).astype(bf16)
    (tok_rel,) = reorder((to_col,), (tok_all,), (CHUNKS,))
    tok_rel = tok_rel.reshape(2048, 384)
    grad_w_in = contract(tok_rel, jnp.concatenate(pregrad_all), 0, 0)
    grad_w_in = (grad_w_in * grad_scale).astype(bf16)
    return (grad_tokens, grad_w_in, grad_w_out)


def solution(mesh):
    fine = Mesh(mesh.devices.reshape(2, 4, 2, 4, 4), ROW + COL)
    in_specs = (P(ROW, COL), P(ROW, COL), P(COL, ROW), P(COL, ROW), P(ROW, COL))
    out_specs = (P(ROW, COL), P(COL, ROW), P(ROW, COL))
    return jax.shard_map(body, mesh=fine, in_specs=in_specs, out_specs=out_specs, check_vma=False)
```

```python
import math

import jax
import jax.numpy as jnp
from jax import lax
from jax.experimental import pallas as pl
from jax.experimental.pallas import tpu as pltpu
from jax.sharding import Mesh
from jax.sharding import PartitionSpec as P

gelu_coef = math.sqrt(2.0 / math.pi)
cubic_coef = 0.044715
ROW = ("zl", "x", "c")
COL = ("zh", "y")
SIZES = {"zl": 2, "x": 4, "c": 2, "zh": 4, "y": 4}
ROWS = 128
ANCHOR = 2 * 10**10
SHORT = (8, 9)
WIDE = 768


def gelu_parts(pre_values):
    pre_f32 = pre_values.astype(jnp.float32)
    tangent = jnp.tanh(gelu_coef * (pre_f32 + cubic_coef * pre_f32 * pre_f32 * pre_f32))
    activated = 0.5 * pre_f32 * (1.0 + tangent)
    slopes = 0.5 * (1.0 + tangent) + 0.5 * pre_f32 * (1.0 - tangent * tangent) * gelu_coef * (
        1.0 + 3.0 * cubic_coef * pre_f32 * pre_f32
    )
    return (activated, slopes)


def contract(left_side, right_side, left_dim, right_dim):
    return lax.dot_general(
        left_side,
        right_side,
        (((left_dim,), (right_dim,)), ((), ())),
        preferred_element_type=jnp.float32,
    )


def shift(values, axis, step):
    if step is None:
        return lax.all_to_all(values, axis, 0, 0, tiled=True)
    size = SIZES[axis]
    return lax.ppermute(values, axis, [(i, (i + step) % size) for i in range(size)])


def fence(*values):
    return lax.optimization_barrier(values)


def place_blocks(index_ref, near_ref, far_ref, *out_refs):
    for t, out_ref in enumerate(out_refs):
        for k in range(8):
            out_ref[index_ref[t, k]] = near_ref[k]
            out_ref[index_ref[t, k + 8]] = far_ref[k]


def reorder(index, near, far):
    shape = jax.ShapeDtypeStruct((16, ROWS, 384), jnp.bfloat16)
    found = pl.pallas_call(
        place_blocks,
        in_specs=[pl.BlockSpec(memory_space=pltpu.SMEM)] + [pl.BlockSpec(memory_space=pltpu.VMEM)] * 2,
        out_specs=[pl.BlockSpec(memory_space=pltpu.VMEM)] * len(index),
        out_shape=[shape] * len(index),
        compiler_params=pltpu.CompilerParams(vmem_limit_bytes=16 * 2**20),
        cost_estimate=pl.CostEstimate(
            flops=0, bytes_accessed=2 * 16 * ROWS * 384 * (1 + len(index)), transcendentals=0
        ),
    )(jnp.stack(index), near, far)
    return [f.reshape(4, 4 * ROWS, 384) for f in found]


def add_blocks(index_ref, a_ref, b_ref, *out_refs):
    k = 0
    for out_ref in out_refs:
        for place in range(out_ref.shape[0]):
            both = a_ref[index_ref[0, k]].astype(jnp.float32) + b_ref[index_ref[1, k]].astype(jnp.float32)
            out_ref[place] = both.astype(jnp.bfloat16)
            k += 1


def combine(index, a, b):
    half = jax.ShapeDtypeStruct((8,) + a.shape[1:], jnp.bfloat16)
    return pl.pallas_call(
        add_blocks,
        in_specs=[pl.BlockSpec(memory_space=pltpu.SMEM)] + [pl.BlockSpec(memory_space=pltpu.VMEM)] * 2,
        out_specs=[pl.BlockSpec(memory_space=pltpu.VMEM)] * 2,
        out_shape=[half, half],
        compiler_params=pltpu.CompilerParams(vmem_limit_bytes=16 * 2**20),
        cost_estimate=pl.CostEstimate(flops=a.size, bytes_accessed=6 * a.size, transcendentals=0),
    )(jnp.stack(index), a, b)


def places():
    zl, x, c, zh, y = (lax.axis_index(n) for n in ROW + COL)

    def orders(dc, dzl, dx):
        block = ((zl + dzl) % 2 * 4 + (x + dx) % 4) * 2 + (c + dc) % 2
        dy = (block % 4 - y) % 4
        return dy * 4 + block // 4, dy * 4 + (block // 4 - zh) % 4

    near = [orders(dc, dzl, dx) for dc in range(2) for dzl in range(2) for dx in range(4)]
    return [jnp.stack(v).astype(jnp.int32) for v in zip(*near)]


def keep_mark(mark_ref, out_ref):
    out_ref[...] = mark_ref[...]


def pass_mark(mark, flops):
    return pl.pallas_call(
        keep_mark,
        out_shape=jax.ShapeDtypeStruct(mark.shape, mark.dtype),
        cost_estimate=pl.CostEstimate(flops=flops, bytes_accessed=0, transcendentals=0),
    )(mark)


def drive(lanes, mark):
    asked, count = [next(lane) for lane in lanes], 0
    while lanes:
        sends = [send for more, _ in asked for send in more]
        inputs = [value for _, more in asked for value in more]
        held = fence(*[values for values, _, _ in sends], *inputs, mark)
        came = [shift(v, axis, step) for v, (_, axis, step) in zip(held, sends)]
        count += 1
        mark = pass_mark(held[-1], 0 if count in SHORT else ANCHOR)
        *held, mark = fence(*held[len(sends) : -1], mark)
        ends = []
        for lane, (more, values) in zip(lanes, asked):
            ends.append(lane.send((came[: len(more)], held[: len(values)])))
            came, held = came[len(more) :], held[len(values) :]
        *flat, mark = fence(*[value for end in ends for value in end], mark)
        going = []
        for lane, end in zip(lanes, ends):
            mine, flat = flat[: len(end)], flat[len(end) :]
            try:
                going.append((lane, lane.send(mine)))
            except StopIteration:
                pass
        lanes, asked = [lane for lane, _ in going], [ask for _, ask in going]


def idle(steps):
    for _ in range(steps):
        yield [], []
        yield []


def halves(values):
    cut = values.shape[1] // 2
    return values[:, :cut], values[:, cut:]


def total(*terms):
    return sum(t.astype(jnp.float32) for t in terms)


def with_half(values, half, side):
    parts = list(halves(values))
    parts[side] = total(parts[side], half).astype(jnp.bfloat16)
    return jnp.concatenate(parts, axis=1)


def post(sends, steps):
    came, _ = yield sends, []
    if steps > 1:
        yield []
        yield from idle(steps - 2)
        yield [], []
    return (yield came)


def post_swap(values, axis, steps):
    (came,) = yield from post([(values, axis, None)], steps)
    return came


def four(values):
    return jnp.stack([values] * 4)


def whole(pair):
    return jnp.concatenate(pair, axis=1)


def body(tokens, out_grad, pre_act, w_in, w_out):
    orders = places()
    bf16 = jnp.bfloat16
    f32 = jnp.float32
    grad_scale = float(2048) ** (-0.5)
    activated, slopes = gelu_parts(pre_act)
    activated = activated.astype(bf16)
    streams = (slice(0, WIDE), slice(WIDE, None))
    made = {}

    def row_gather(own, pause):
        (other,) = yield from post([(own, "zl", 1)], 1)
        yield from idle(pause)
        pair = jnp.stack([own, other])
        came = yield from post([(pair, "x", -1), (pair, "x", 2), (pair, "x", 1)], 1)
        chip = jnp.stack([pair] + came, axis=1).reshape(8, ROWS, 384)
        yield from idle((pause + 1) // 2)
        (far,) = yield from post([(chip, "c", 1)], 1)
        return reorder(orders, chip, far)

    def lane_grad():
        made["grad"] = yield from row_gather(out_grad, 0)

    def lane_tokens():
        yield from idle(1)
        made["tok"] = yield from row_gather(tokens, 5)

    def scatter_y(stream):
        grad, weight = made["grad"][stream], w_out[streams[stream]]

        def far_halves(rows):
            return [contract(rows, half, 1, 1).astype(bf16) for half in jnp.split(weight, 2)]

        if stream == 0:
            first, second = far_halves(grad[2])
        else:
            _, held = yield [], [grad[2]]
            first, second = yield far_halves(held[0])
        came, rows = yield [(first, "y", 1), (second, "y", -1)], [grad[1], grad[3]]
        near = yield [contract(r, weight, 1, 1).astype(bf16) for r in rows]
        yield [], []
        came = yield came
        up, down = with_half(near[0], came[0], 0), with_half(near[1], came[1], 1)
        came, rows = yield [(up, "y", 1), (down, "y", -1)], [grad[0]]
        (own,) = yield [contract(rows[0], weight, 1, 1).astype(bf16)]
        yield [], []
        came = yield came
        return total(own, *came)

    def gather_y(stream, near):
        weight = w_in[:, streams[stream]]

        def part(piece):
            return contract(piece, weight, 1, 1).astype(bf16)

        came, held = yield [(near, "y", 1), (near, "y", -1)], [near]
        left, right, first = yield came + [part(held[0])]
        sends = [(halves(left)[0], "y", 1), (halves(right)[1], "y", -1)]
        came, held = yield sends, [right, left]
        *far, after, before = yield came + [part(h) for h in held]
        made["found", stream] = (near, right, whole(far), left)
        made["parts", stream] = jnp.stack([first, after, part(whole(far)), before]).reshape(16, ROWS, 384)

    def token_grads(stream, pieces, places_now):
        return sum(contract(made["tok"][stream][dy], p, 0, 0) for dy, p in zip(places_now, pieces))

    def lane_first():
        yield from idle(3)
        sums = (yield from scatter_y(0)).astype(bf16)
        came = yield from post_swap(sums.reshape(4, ROWS, -1), "zh", 2)
        pregrad = (jnp.sum(came.astype(f32), axis=0) * slopes[:, streams[0]]).astype(bf16)
        near = (yield from post_swap(four(pregrad), "zh", 1)).reshape(4 * ROWS, -1)
        yield from gather_y(0, near)
        _, held = yield [], [*made["found", 0], made["parts", 0]]
        done = yield [token_grads(0, held[:4], range(4)), held[4]]
        made["w_in", 0], made["parts", 0] = done

    def lane_second():
        yield from idle(3)
        sums = yield from scatter_y(1)
        yield from idle(1)
        rows = [sums[dz * ROWS : (dz + 1) * ROWS] for dz in range(4)]
        came = yield from post([(rows[dz].astype(bf16), "zh", dz) for dz in (1, 2, 3)], 1)
        pregrad = (total(rows[0], *came) * slopes[:, streams[1]]).astype(bf16)
        came = yield from post([(pregrad, "zh", -dz) for dz in (1, 2, 3)], 1)
        near = jnp.concatenate([pregrad] + came)
        yield from gather_y(1, near)

    def lane_act():
        yield from idle(3)
        _, held = yield [], [activated]
        near = shift(four(held[0]), "zh", None)
        yield []
        yield from idle(2)
        yield [], []
        (near,) = yield [near]
        near = near.reshape(4 * ROWS, -1)
        yield from idle(2)
        left, right = yield from post([(near, "y", 1), (near, "y", -1)], 1)
        grad = made["grad"][0]
        _, held = yield [], [near]
        (sums,) = yield [contract(held[0], grad[0], 0, 0)]
        _, held = yield [], [right, left]
        (sums,) = yield [sums + contract(held[0], grad[1], 0, 0) + contract(held[1], grad[3], 0, 0)]
        _, held = yield [], [left, right]
        ends = yield [halves(held[0])[0], halves(held[1])[1]]
        far = yield from post([(ends[0], "y", 1), (ends[1], "y", -1)], 3)
        grad = sums + contract(whole(far), grad[2], 0, 0)
        made["w_out"] = (grad * grad_scale).astype(bf16)

    def lane_row():
        yield from idle(13)
        keep, give = combine(orders, made["parts", 0], made["parts", 1])
        found = made["found", 1]
        came, held = yield [(give, "c", 1)], [found[0], found[1]]
        came, sums = yield came + [token_grads(1, held, (0, 1))]
        mine = total(keep, came).astype(bf16).reshape(2, 4, ROWS, 384)
        came, held = yield [(mine[:, dx], "x", dx) for dx in (1, 2, 3)], [found[2], found[3]]
        *came, sums = yield came + [sums + token_grads(1, held, (2, 3))]
        both = total(mine[:, 0], *came)
        came, held = yield [(both[1].astype(bf16), "zl", 1)], [made["w_in", 0], sums]
        came, made["w_in"] = yield came + [(whole(held) * grad_scale).astype(bf16)]
        made["tokens"] = total(both[0], came).astype(bf16)

    mark = pre_act[:8, :128].astype(f32)
    drive([lane_grad(), lane_tokens(), lane_act(), lane_first(), lane_second(), lane_row()], mark)
    return (made["tokens"], made["w_in"], made["w_out"])


def solution(mesh):
    fine = Mesh(mesh.devices.reshape(2, 4, 2, 4, 4), ROW + COL)
    in_specs = (P(ROW, COL), P(ROW, COL), P(COL, ROW), P(COL, ROW), P(ROW, COL))
    out_specs = (P(ROW, COL), P(COL, ROW), P(ROW, COL))
    return jax.shard_map(body, mesh=fine, in_specs=in_specs, out_specs=out_specs, check_vma=False)
```

```python
import functools
import math

import jax
import jax.numpy as jnp
from jax import lax
from jax.experimental import pallas as pl
from jax.experimental.pallas import tpu as pltpu
from jax.sharding import Mesh
from jax.sharding import PartitionSpec as P

gelu_coef = math.sqrt(2.0 / math.pi)
cubic_coef = 0.044715
ROW = ("zl", "x", "c")
COL = ("zh", "y")
SIZES = {"zl": 2, "x": 4, "c": 2, "zh": 4, "y": 4}
ROWS = 128
ANCHOR = 2 * 10**10
SHORT = (3, 7)
WIDE = 768


def gelu_parts(pre_values):
    pre_f32 = pre_values.astype(jnp.float32)
    tangent = jnp.tanh(gelu_coef * (pre_f32 + cubic_coef * pre_f32 * pre_f32 * pre_f32))
    activated = 0.5 * pre_f32 * (1.0 + tangent)
    slopes = 0.5 * (1.0 + tangent) + 0.5 * pre_f32 * (1.0 - tangent * tangent) * gelu_coef * (
        1.0 + 3.0 * cubic_coef * pre_f32 * pre_f32
    )
    return (activated, slopes)


def contract(left_side, right_side, left_dim, right_dim):
    return lax.dot_general(
        left_side,
        right_side,
        (((left_dim,), (right_dim,)), ((), ())),
        preferred_element_type=jnp.float32,
    )


def shift(values, axis, step):
    if step is None:
        return lax.all_to_all(values, axis, 0, 0, tiled=True)
    size = SIZES[axis]
    return lax.ppermute(values, axis, [(i, (i + step) % size) for i in range(size)])


def fence(*values):
    return lax.optimization_barrier(values)


def place_blocks(index_ref, near_ref, far_ref, *out_refs):
    for t, out_ref in enumerate(out_refs):
        for k in range(8):
            out_ref[index_ref[t, k]] = near_ref[k]
            out_ref[index_ref[t, k + 8]] = far_ref[k]


def reorder(index, near, far):
    shape = jax.ShapeDtypeStruct((16, ROWS, 384), jnp.bfloat16)
    found = pl.pallas_call(
        place_blocks,
        in_specs=[pl.BlockSpec(memory_space=pltpu.SMEM)] + [pl.BlockSpec(memory_space=pltpu.VMEM)] * 2,
        out_specs=[pl.BlockSpec(memory_space=pltpu.VMEM)] * len(index),
        out_shape=[shape] * len(index),
        compiler_params=pltpu.CompilerParams(vmem_limit_bytes=16 * 2**20),
        cost_estimate=pl.CostEstimate(
            flops=0, bytes_accessed=2 * 16 * ROWS * 384 * (1 + len(index)), transcendentals=0
        ),
    )(jnp.stack(index), near, far)
    return [f.reshape(4, 4 * ROWS, 384) for f in found]


def add_blocks(index_ref, a_ref, b_ref, *out_refs):
    k = 0
    for out_ref in out_refs:
        for place in range(out_ref.shape[0]):
            both = a_ref[index_ref[0, k]].astype(jnp.float32) + b_ref[index_ref[1, k]].astype(jnp.float32)
            out_ref[place] = both.astype(jnp.bfloat16)
            k += 1


def combine(index, a, b):
    half = jax.ShapeDtypeStruct((8,) + a.shape[1:], jnp.bfloat16)
    return pl.pallas_call(
        add_blocks,
        in_specs=[pl.BlockSpec(memory_space=pltpu.SMEM)] + [pl.BlockSpec(memory_space=pltpu.VMEM)] * 2,
        out_specs=[pl.BlockSpec(memory_space=pltpu.VMEM)] * 2,
        out_shape=[half, half],
        compiler_params=pltpu.CompilerParams(vmem_limit_bytes=16 * 2**20),
        cost_estimate=pl.CostEstimate(flops=a.size, bytes_accessed=6 * a.size, transcendentals=0),
    )(jnp.stack(index), a, b)


def add_products(count, scale, *refs):
    out_ref = refs[-1]
    total_now = None
    for k in range(count):
        more = lax.dot_general(
            refs[k][...],
            refs[count + k][...],
            (((0,), (0,)), ((), ())),
            preferred_element_type=jnp.float32,
        )
        total_now = more if total_now is None else total_now + more
    if len(refs) > 2 * count + 1:
        total_now = total_now + refs[2 * count][...]
    out_ref[...] = (total_now * scale).astype(out_ref.dtype)


def weight_grad(pieces, rows, before, scale, dtype):
    columns, width = pieces[0].shape[1], rows[0].shape[1]
    wide = pl.BlockSpec((pieces[0].shape[0], 256), lambda i: (0, i))
    out = pl.BlockSpec((256, width), lambda i: (i, 0))
    return pl.pallas_call(
        functools.partial(add_products, len(pieces), scale),
        grid=(columns // 256,),
        in_specs=[wide] * len(pieces)
        + [pl.BlockSpec(rows[0].shape, lambda i: (0, 0))] * len(rows)
        + [out] * len(before),
        out_specs=out,
        out_shape=jax.ShapeDtypeStruct((columns, width), dtype),
        compiler_params=pltpu.CompilerParams(vmem_limit_bytes=24 * 2**20),
        cost_estimate=pl.CostEstimate(flops=0, bytes_accessed=0, transcendentals=0),
    )(*pieces, *rows, *before)


def places():
    zl, x, c, zh, y = (lax.axis_index(n) for n in ROW + COL)

    def orders(dc, dzl, dx):
        block = ((zl + dzl) % 2 * 4 + (x + dx) % 4) * 2 + (c + dc) % 2
        dy = (block % 4 - y) % 4
        return dy * 4 + block // 4, dy * 4 + (block // 4 - zh) % 4

    near = [orders(dc, dzl, dx) for dc in range(2) for dzl in range(2) for dx in range(4)]
    return [jnp.stack(v).astype(jnp.int32) for v in zip(*near)]


def keep_mark(mark_ref, out_ref):
    out_ref[...] = mark_ref[...]


def pass_mark(mark, flops):
    return pl.pallas_call(
        keep_mark,
        out_shape=jax.ShapeDtypeStruct(mark.shape, mark.dtype),
        cost_estimate=pl.CostEstimate(flops=flops, bytes_accessed=0, transcendentals=0),
    )(mark)


def drive(lanes, mark):
    asked, count = [next(lane) for lane in lanes], 0
    while lanes:
        sends = [send for more, _ in asked for send in more]
        inputs = [value for _, more in asked for value in more]
        held = fence(*[values for values, _, _ in sends], *inputs, mark)
        came = [shift(v, axis, step) for v, (_, axis, step) in zip(held, sends)]
        count += 1
        mark = pass_mark(held[-1], 0 if count in SHORT else ANCHOR)
        *held, mark = fence(*held[len(sends) : -1], mark)
        ends = []
        for lane, (more, values) in zip(lanes, asked):
            ends.append(lane.send((came[: len(more)], held[: len(values)])))
            came, held = came[len(more) :], held[len(values) :]
        *flat, mark = fence(*[value for end in ends for value in end], mark)
        going = []
        for lane, end in zip(lanes, ends):
            mine, flat = flat[: len(end)], flat[len(end) :]
            try:
                going.append((lane, lane.send(mine)))
            except StopIteration:
                pass
        lanes, asked = [lane for lane, _ in going], [ask for _, ask in going]


def idle(steps):
    for _ in range(steps):
        yield [], []
        yield []


def halves(values):
    cut = values.shape[1] // 2
    return values[:, :cut], values[:, cut:]


def total(*terms):
    return sum(t.astype(jnp.float32) for t in terms)


def with_half(values, half, side):
    parts = list(halves(values))
    parts[side] = total(parts[side], half).astype(jnp.bfloat16)
    return jnp.concatenate(parts, axis=1)


def post(sends, steps):
    came, _ = yield sends, []
    if steps > 1:
        yield []
        yield from idle(steps - 2)
        yield [], []
    return (yield came)


def post_swap(values, axis, steps):
    (came,) = yield from post([(values, axis, None)], steps)
    return came


def four(values):
    return jnp.stack([values] * 4)


def whole(pair):
    return jnp.concatenate(pair, axis=1)


def body(tokens, out_grad, pre_act, w_in, w_out):
    orders = places()
    bf16 = jnp.bfloat16
    f32 = jnp.float32
    grad_scale = float(2048) ** (-0.5)
    streams = (slice(0, WIDE), slice(WIDE, None))
    made = {}

    def row_gather(own, pause):
        (other,) = yield from post([(own, "zl", 1)], 1)
        yield from idle(pause)
        pair = jnp.stack([own, other])
        came = yield from post([(pair, "x", -1), (pair, "x", 2), (pair, "x", 1)], 1)
        chip = jnp.stack([pair] + came, axis=1).reshape(8, ROWS, 384)
        yield from idle(pause and 4)
        (far,) = yield from post([(chip, "c", 1)], 1)
        return reorder(orders, chip, far)

    def lane_grad():
        made["grad"] = yield from row_gather(out_grad, 0)

    def lane_tokens():
        made["tok"] = yield from row_gather(tokens, 3)

    def scatter_y(stream):
        grad, weight = made["grad"][stream], w_out[streams[stream]]

        def far_halves(rows):
            return [contract(rows, half, 1, 1).astype(bf16) for half in jnp.split(weight, 2)]

        first, second = far_halves(grad[2])
        came, rows = yield [(first, "y", 1), (second, "y", -1)], [grad[1], grad[3]]
        came = yield came + [contract(r, weight, 1, 1).astype(bf16) for r in rows]
        if stream == 1:
            _, came = yield [], came
        up, down = with_half(came[2], came[0], 0), with_half(came[3], came[1], 1)
        if stream == 1:
            up, down = yield [up, down]
        came, rows = yield [(up, "y", 1), (down, "y", -1)], [grad[0]]
        came = yield came + [contract(rows[0], weight, 1, 1).astype(bf16)]
        return total(*came)

    def gather_y(stream, near):
        weight = w_in[:, streams[stream]]

        def part(piece):
            return contract(piece, weight, 1, 1).astype(bf16)

        came, held = yield [(near, "y", 1), (near, "y", -1)], [near]
        left, right, first = yield came + [part(held[0])]
        sends = [(halves(left)[0], "y", 1), (halves(right)[1], "y", -1)]
        came, held = yield sends, [right, left]
        *far, after, before = yield came + [part(h) for h in held]
        made["found", stream] = (near, right, whole(far), left)
        made["parts", stream] = jnp.stack([first, after, part(whole(far)), before]).reshape(16, ROWS, 384)

    def token_grads(stream, pieces, places_now):
        return sum(contract(made["tok"][stream][dy], p, 0, 0) for dy, p in zip(places_now, pieces))

    def lane_first():
        yield from idle(3)
        sums = (yield from scatter_y(0)).astype(bf16)
        came = yield from post_swap(sums.reshape(4, ROWS, -1), "zh", 2)
        pregrad = (jnp.sum(came.astype(f32), axis=0) * made["slopes"][:, streams[0]]).astype(bf16)
        near = (yield from post_swap(four(pregrad), "zh", 1)).reshape(4 * ROWS, -1)
        yield from gather_y(0, near)
        _, held = yield [], [*made["found", 0], made["parts", 0]]
        done = yield [token_grads(0, held[:4], range(4)), held[4]]
        made["w_in", 0], made["parts", 0] = done

    def lane_second():
        yield from idle(3)
        sums = yield from scatter_y(1)
        rows = [sums[dz * ROWS : (dz + 1) * ROWS] for dz in range(4)]
        came = yield from post([(rows[dz].astype(bf16), "zh", dz) for dz in (1, 2, 3)], 1)
        yield from idle(1)
        pregrad = (total(rows[0], *came) * made["slopes"][:, streams[1]]).astype(bf16)
        came = yield from post([(pregrad, "zh", -dz) for dz in (1, 2, 3)], 1)
        near = jnp.concatenate([pregrad] + came)
        yield from gather_y(1, near)

    def lane_act():
        _, held = yield [], [pre_act]
        activated, made["slopes"] = gelu_parts(held[0])
        copies, made["slopes"] = yield [four(activated.astype(bf16)), made["slopes"]]
        _, held = yield [], [copies]
        near = shift(held[0], "zh", None)
        yield []
        yield from idle(2)
        yield [], []
        (near,) = yield [near]
        near = near.reshape(4 * ROWS, -1)
        yield from idle(1)
        grad = made["grad"][0]
        came, _ = yield [(near, "y", 1), (near, "y", -1)], []
        yield []
        yield [], []
        left, right = yield came
        yield from idle(1)
        _, held = yield [], [near, right, left]
        rows = [grad[dy] for dy in (0, 1, 3)]
        ends = [halves(held[2])[0], halves(held[1])[1]]
        *ends, sums = yield ends + [weight_grad(held, rows, [], 1.0, f32)]
        yield from idle(1)
        far = yield from post([(ends[0], "y", 1), (ends[1], "y", -1)], 3)
        made["w_out"] = weight_grad([whole(far)], [grad[2]], [sums], grad_scale, bf16)

    def lane_row():
        yield from idle(11)
        keep, give = combine(orders, made["parts", 0], made["parts", 1])
        found = made["found", 1]
        came, held = yield [(give, "c", 1)], [found[0], found[1]]
        came, sums = yield came + [token_grads(1, held, (0, 1))]
        mine = total(keep, came).astype(bf16).reshape(2, 4, ROWS, 384)
        came, held = yield [(mine[:, dx], "x", dx) for dx in (1, 2, 3)], [found[2], found[3]]
        *came, sums = yield came + [sums + token_grads(1, held, (2, 3))]
        both = total(mine[:, 0], *came)
        came, held = yield [(both[1].astype(bf16), "zl", 1)], [made["w_in", 0], sums]
        came, made["w_in"] = yield came + [(whole(held) * grad_scale).astype(bf16)]
        made["tokens"] = total(both[0], came).astype(bf16)

    mark = pre_act[:8, :128].astype(f32)
    drive([lane_grad(), lane_tokens(), lane_act(), lane_first(), lane_second(), lane_row()], mark)
    return (made["tokens"], made["w_in"], made["w_out"])


def solution(mesh):
    fine = Mesh(mesh.devices.reshape(2, 4, 2, 4, 4), ROW + COL)
    in_specs = (P(ROW, COL), P(ROW, COL), P(COL, ROW), P(COL, ROW), P(ROW, COL))
    out_specs = (P(ROW, COL), P(COL, ROW), P(ROW, COL))
    return jax.shard_map(body, mesh=fine, in_specs=in_specs, out_specs=out_specs, check_vma=False)
```

```python
import functools
import math

import jax
import jax.numpy as jnp
from jax import lax
from jax.experimental import pallas as pl
from jax.experimental.pallas import tpu as pltpu
from jax.sharding import Mesh
from jax.sharding import PartitionSpec as P

gelu_coef = math.sqrt(2.0 / math.pi)
cubic_coef = 0.044715
ROW = ("zl", "x", "c")
COL = ("zh", "y")
SIZES = {"zl": 2, "x": 4, "c": 2, "zh": 4, "y": 4}
ROWS = 128
ANCHOR = 2 * 10**10
SHORT = (7,)
WIDE = 768


def gelu_parts(pre_values):
    pre_f32 = pre_values.astype(jnp.float32)
    tangent = jnp.tanh(gelu_coef * (pre_f32 + cubic_coef * pre_f32 * pre_f32 * pre_f32))
    activated = 0.5 * pre_f32 * (1.0 + tangent)
    slopes = 0.5 * (1.0 + tangent) + 0.5 * pre_f32 * (1.0 - tangent * tangent) * gelu_coef * (
        1.0 + 3.0 * cubic_coef * pre_f32 * pre_f32
    )
    return (activated, slopes)


def contract(left_side, right_side, left_dim, right_dim):
    return lax.dot_general(
        left_side,
        right_side,
        (((left_dim,), (right_dim,)), ((), ())),
        preferred_element_type=jnp.float32,
    )


def shift(values, axis, step):
    if step is None:
        return lax.all_to_all(values, axis, 0, 0, tiled=True)
    size = SIZES[axis]
    return lax.ppermute(values, axis, [(i, (i + step) % size) for i in range(size)])


def fence(*values):
    return lax.optimization_barrier(values)


def place_blocks(index_ref, near_ref, far_ref, *out_refs):
    for t, out_ref in enumerate(out_refs):
        for k in range(8):
            out_ref[index_ref[t, k]] = near_ref[k]
            out_ref[index_ref[t, k + 8]] = far_ref[k]


def reorder(index, near, far):
    shape = jax.ShapeDtypeStruct((16, ROWS, 384), jnp.bfloat16)
    found = pl.pallas_call(
        place_blocks,
        in_specs=[pl.BlockSpec(memory_space=pltpu.SMEM)] + [pl.BlockSpec(memory_space=pltpu.VMEM)] * 2,
        out_specs=[pl.BlockSpec(memory_space=pltpu.VMEM)] * len(index),
        out_shape=[shape] * len(index),
        compiler_params=pltpu.CompilerParams(vmem_limit_bytes=16 * 2**20),
        cost_estimate=pl.CostEstimate(
            flops=0, bytes_accessed=2 * 16 * ROWS * 384 * (1 + len(index)), transcendentals=0
        ),
    )(jnp.stack(index), near, far)
    return [f.reshape(4, 4 * ROWS, 384) for f in found]


def add_blocks(index_ref, a_ref, b_ref, *out_refs):
    k = 0
    for out_ref in out_refs:
        for place in range(out_ref.shape[0]):
            both = a_ref[index_ref[0, k]].astype(jnp.float32) + b_ref[index_ref[1, k]].astype(jnp.float32)
            out_ref[place] = both.astype(jnp.bfloat16)
            k += 1


def combine(index, a, b):
    half = jax.ShapeDtypeStruct((8,) + a.shape[1:], jnp.bfloat16)
    return pl.pallas_call(
        add_blocks,
        in_specs=[pl.BlockSpec(memory_space=pltpu.SMEM)] + [pl.BlockSpec(memory_space=pltpu.VMEM)] * 2,
        out_specs=[pl.BlockSpec(memory_space=pltpu.VMEM)] * 2,
        out_shape=[half, half],
        compiler_params=pltpu.CompilerParams(vmem_limit_bytes=16 * 2**20),
        cost_estimate=pl.CostEstimate(flops=a.size, bytes_accessed=6 * a.size, transcendentals=0),
    )(jnp.stack(index), a, b)


def add_products(count, scale, *refs):
    out_ref = refs[-1]
    total_now = None
    for k in range(count):
        more = lax.dot_general(
            refs[k][...],
            refs[count + k][...],
            (((0,), (0,)), ((), ())),
            preferred_element_type=jnp.float32,
        )
        total_now = more if total_now is None else total_now + more
    if len(refs) > 2 * count + 1:
        total_now = total_now + refs[2 * count][...]
    out_ref[...] = (total_now * scale).astype(out_ref.dtype)


def weight_grad(pieces, rows, before, scale, dtype):
    columns, width = pieces[0].shape[1], rows[0].shape[1]
    wide = pl.BlockSpec((pieces[0].shape[0], 256), lambda i: (0, i))
    out = pl.BlockSpec((256, width), lambda i: (i, 0))
    return pl.pallas_call(
        functools.partial(add_products, len(pieces), scale),
        grid=(columns // 256,),
        in_specs=[wide] * len(pieces)
        + [pl.BlockSpec(rows[0].shape, lambda i: (0, 0))] * len(rows)
        + [out] * len(before),
        out_specs=out,
        out_shape=jax.ShapeDtypeStruct((columns, width), dtype),
        compiler_params=pltpu.CompilerParams(vmem_limit_bytes=24 * 2**20),
        cost_estimate=pl.CostEstimate(flops=0, bytes_accessed=0, transcendentals=0),
    )(*pieces, *rows, *before)


def places():
    zl, x, c, zh, y = (lax.axis_index(n) for n in ROW + COL)

    def orders(dc, dzl, dx):
        block = ((zl + dzl) % 2 * 4 + (x + dx) % 4) * 2 + (c + dc) % 2
        dy = (block % 4 - y) % 4
        return dy * 4 + block // 4, dy * 4 + (block // 4 - zh) % 4

    near = [orders(dc, dzl, dx) for dc in range(2) for dzl in range(2) for dx in range(4)]
    return [jnp.stack(v).astype(jnp.int32) for v in zip(*near)]


def keep_mark(mark_ref, out_ref):
    out_ref[...] = mark_ref[...]


def pass_mark(mark, flops):
    return pl.pallas_call(
        keep_mark,
        out_shape=jax.ShapeDtypeStruct(mark.shape, mark.dtype),
        cost_estimate=pl.CostEstimate(flops=flops, bytes_accessed=0, transcendentals=0),
    )(mark)


def drive(lanes, mark):
    asked, count = [next(lane) for lane in lanes], 0
    while lanes:
        sends = [send for more, _ in asked for send in more]
        inputs = [value for _, more in asked for value in more]
        held = fence(*[values for values, _, _ in sends], *inputs, mark)
        came = [shift(v, axis, step) for v, (_, axis, step) in zip(held, sends)]
        count += 1
        mark = pass_mark(held[-1], 0 if count in SHORT else ANCHOR)
        *held, mark = fence(*held[len(sends) : -1], mark)
        ends = []
        for lane, (more, values) in zip(lanes, asked):
            ends.append(lane.send((came[: len(more)], held[: len(values)])))
            came, held = came[len(more) :], held[len(values) :]
        *flat, mark = fence(*[value for end in ends for value in end], mark)
        going = []
        for lane, end in zip(lanes, ends):
            mine, flat = flat[: len(end)], flat[len(end) :]
            try:
                going.append((lane, lane.send(mine)))
            except StopIteration:
                pass
        lanes, asked = [lane for lane, _ in going], [ask for _, ask in going]


def idle(steps):
    for _ in range(steps):
        yield [], []
        yield []


def halves(values):
    cut = values.shape[1] // 2
    return values[:, :cut], values[:, cut:]


def total(*terms):
    return sum(t.astype(jnp.float32) for t in terms)


def with_half(values, half, side):
    parts = list(halves(values))
    parts[side] = total(parts[side], half).astype(jnp.bfloat16)
    return jnp.concatenate(parts, axis=1)


def post(sends, steps):
    came, _ = yield sends, []
    if steps > 1:
        yield []
        yield from idle(steps - 2)
        yield [], []
    return (yield came)


def post_swap(values, axis, steps):
    (came,) = yield from post([(values, axis, None)], steps)
    return came


def four(values):
    return jnp.stack([values] * 4)


def whole(pair):
    return jnp.concatenate(pair, axis=1)


def body(tokens, out_grad, pre_act, w_in, w_out):
    orders = places()
    bf16 = jnp.bfloat16
    f32 = jnp.float32
    grad_scale = float(2048) ** (-0.5)
    streams = (slice(0, WIDE), slice(WIDE, None))
    made = {}

    def row_gather(own, pause):
        (other,) = yield from post([(own, "zl", 1)], 1)
        yield from idle(pause)
        pair = jnp.stack([own, other])
        came = yield from post([(pair, "x", -1), (pair, "x", 2), (pair, "x", 1)], 1)
        chip = jnp.stack([pair] + came, axis=1).reshape(8, ROWS, 384)
        yield from idle(pause and 4)
        (far,) = yield from post([(chip, "c", 1)], 1)
        return reorder(orders, chip, far)

    def lane_grad():
        made["grad"] = yield from row_gather(out_grad, 0)

    def lane_tokens():
        made["tok"] = yield from row_gather(tokens, 3)

    def scatter_y(stream):
        grad, weight = made["grad"][0], w_out[streams[stream]]
        sends = []
        if stream == 0:
            for step, half in ((1, 0), (-1, 1)):
                rows = jnp.concatenate([jnp.split(w_out[s], 2)[half] for s in streams])
                sends.append((contract(grad[2], rows, 1, 1).astype(bf16), "y", step))
        came, rows = yield sends, [grad[1], grad[3]]
        came = yield came + [contract(r, weight, 1, 1).astype(bf16) for r in rows]
        if stream == 0:
            made["far"] = came[:2]
        else:
            _, came = yield [], list(made["far"]) + came
        up = with_half(came[2], halves(came[0])[stream], 0)
        down = with_half(came[3], halves(came[1])[stream], 1)
        if stream == 1:
            up, down = yield [up, down]
        came, rows = yield [(up, "y", 1), (down, "y", -1)], [grad[0]]
        came = yield came + [contract(rows[0], weight, 1, 1).astype(bf16)]
        return total(*came)

    def gather_y(stream, near):
        weight = w_in[:, streams[stream]]

        def part(piece):
            return contract(piece, weight, 1, 1).astype(bf16)

        came, held = yield [(near, "y", 1), (near, "y", -1)], [near]
        left, right, first = yield came + [part(held[0])]
        sends = [(halves(left)[0], "y", 1), (halves(right)[1], "y", -1)]
        came, held = yield sends, [right, left]
        *far, after, before = yield came + [part(h) for h in held]
        made["found", stream] = (near, right, whole(far), left)
        made["parts", stream] = jnp.stack([first, after, part(whole(far)), before]).reshape(16, ROWS, 384)

    def token_grads(stream, pieces, places_now):
        return sum(contract(made["tok"][stream][dy], p, 0, 0) for dy, p in zip(places_now, pieces))

    def lane_first():
        yield from idle(3)
        sums = (yield from scatter_y(0)).astype(bf16)
        came = yield from post_swap(sums.reshape(4, ROWS, -1), "zh", 2)
        pregrad = (jnp.sum(came.astype(f32), axis=0) * made["slopes"][:, streams[0]]).astype(bf16)
        near = (yield from post_swap(four(pregrad), "zh", 1)).reshape(4 * ROWS, -1)
        yield from gather_y(0, near)
        _, held = yield [], [*made["found", 0], made["parts", 0]]
        done = yield [token_grads(0, held[:4], range(4)), held[4]]
        made["w_in", 0], made["parts", 0] = done

    def lane_second():
        yield from idle(3)
        sums = yield from scatter_y(1)
        here = lax.axis_index("zh")
        rows = [lax.dynamic_slice_in_dim(sums, (here + dz) % 4 * ROWS, ROWS, 0) for dz in range(4)]
        came = yield from post([(rows[dz].astype(bf16), "zh", dz) for dz in (1, 2, 3)], 1)
        yield from idle(1)
        pregrad = (total(rows[0], *came) * made["slopes"][:, streams[1]]).astype(bf16)
        came = yield from post([(pregrad, "zh", -dz) for dz in (1, 2, 3)], 1)
        near = jnp.concatenate([pregrad] + came)
        yield from gather_y(1, near)

    def lane_act():
        _, held = yield [], [pre_act]
        activated, made["slopes"] = gelu_parts(held[0])
        copies, made["slopes"] = yield [four(activated.astype(bf16)), made["slopes"]]
        yield from idle(2)
        _, held = yield [], [copies]
        near = shift(held[0], "zh", None)
        yield []
        yield from idle(1)
        yield [], []
        (near,) = yield [near]
        near = near.reshape(4 * ROWS, -1)
        grad = made["grad"][0]
        came, _ = yield [(near, "y", 1), (near, "y", -1)], []
        yield []
        yield [], []
        left, right = yield came
        yield from idle(1)
        _, held = yield [], [near, right, left]
        rows = [grad[dy] for dy in (0, 1, 3)]
        ends = [halves(held[2])[0], halves(held[1])[1]]
        *ends, sums = yield ends + [weight_grad(held, rows, [], 1.0, f32)]
        yield from idle(1)
        far = yield from post([(ends[0], "y", 1), (ends[1], "y", -1)], 3)
        made["w_out"] = weight_grad([whole(far)], [grad[2]], [sums], grad_scale, bf16)

    def lane_row():
        yield from idle(11)
        keep, give = combine(orders, made["parts", 0], made["parts", 1])
        found = made["found", 1]
        came, held = yield [(give, "c", 1)], [found[0], found[1]]
        came, sums = yield came + [token_grads(1, held, (0, 1))]
        mine = total(keep, came).astype(bf16).reshape(2, 4, ROWS, 384)
        came, held = yield [(mine[:, dx], "x", dx) for dx in (1, 2, 3)], [found[2], found[3]]
        *came, sums = yield came + [sums + token_grads(1, held, (2, 3))]
        both = total(mine[:, 0], *came)
        came, held = yield [(both[1].astype(bf16), "zl", 1)], [made["w_in", 0], sums]
        came, made["w_in"] = yield came + [(whole(held) * grad_scale).astype(bf16)]
        made["tokens"] = total(both[0], came).astype(bf16)

    mark = pre_act[:8, :128].astype(f32)
    drive([lane_grad(), lane_tokens(), lane_act(), lane_first(), lane_second(), lane_row()], mark)
    return (made["tokens"], made["w_in"], made["w_out"])


def solution(mesh):
    fine = Mesh(mesh.devices.reshape(2, 4, 2, 4, 4), ROW + COL)
    in_specs = (P(ROW, COL), P(ROW, COL), P(COL, ROW), P(COL, ROW), P(ROW, COL))
    out_specs = (P(ROW, COL), P(COL, ROW), P(ROW, COL))
    return jax.shard_map(body, mesh=fine, in_specs=in_specs, out_specs=out_specs, check_vma=False)
```

```python
import functools
import math

import jax
import jax.numpy as jnp
from jax import lax
from jax.experimental import pallas as pl
from jax.experimental.pallas import tpu as pltpu
from jax.sharding import Mesh
from jax.sharding import PartitionSpec as P

gelu_coef = math.sqrt(2.0 / math.pi)
cubic_coef = 0.044715
ROW = ("zl", "x", "c")
COL = ("zh", "y")
SIZES = {"zl": 2, "x": 4, "c": 2, "zh": 4, "y": 4}
ROWS = 128
ANCHOR = 2 * 10**10
SHORT = (7,)
WIDE = 768


def gelu_parts(pre_values):
    pre_f32 = pre_values.astype(jnp.float32)
    tangent = jnp.tanh(gelu_coef * (pre_f32 + cubic_coef * pre_f32 * pre_f32 * pre_f32))
    activated = 0.5 * pre_f32 * (1.0 + tangent)
    slopes = 0.5 * (1.0 + tangent) + 0.5 * pre_f32 * (1.0 - tangent * tangent) * gelu_coef * (
        1.0 + 3.0 * cubic_coef * pre_f32 * pre_f32
    )
    return (activated, slopes)


def contract(left_side, right_side, left_dim, right_dim):
    return lax.dot_general(
        left_side,
        right_side,
        (((left_dim,), (right_dim,)), ((), ())),
        preferred_element_type=jnp.float32,
    )


def shift(values, axis, step):
    if step is None:
        return lax.all_to_all(values, axis, 0, 0, tiled=True)
    size = SIZES[axis]
    return lax.ppermute(values, axis, [(i, (i + step) % size) for i in range(size)])


def fence(*values):
    return lax.optimization_barrier(values)


def place_blocks(index_ref, near_ref, far_ref, *out_refs):
    for t, out_ref in enumerate(out_refs):
        for k in range(8):
            out_ref[index_ref[t, k]] = near_ref[k]
            out_ref[index_ref[t, k + 8]] = far_ref[k]


def reorder(index, near, far):
    shape = jax.ShapeDtypeStruct((16, ROWS, 384), jnp.bfloat16)
    found = pl.pallas_call(
        place_blocks,
        in_specs=[pl.BlockSpec(memory_space=pltpu.SMEM)] + [pl.BlockSpec(memory_space=pltpu.VMEM)] * 2,
        out_specs=[pl.BlockSpec(memory_space=pltpu.VMEM)] * len(index),
        out_shape=[shape] * len(index),
        compiler_params=pltpu.CompilerParams(vmem_limit_bytes=16 * 2**20),
        cost_estimate=pl.CostEstimate(
            flops=0, bytes_accessed=2 * 16 * ROWS * 384 * (1 + len(index)), transcendentals=0
        ),
    )(jnp.stack(index), near, far)
    return [f.reshape(4, 4 * ROWS, 384) for f in found]


def add_blocks(index_ref, a_ref, b_ref, *out_refs):
    k = 0
    for out_ref in out_refs:
        for place in range(out_ref.shape[0]):
            both = a_ref[index_ref[0, k]].astype(jnp.float32) + b_ref[index_ref[1, k]].astype(jnp.float32)
            out_ref[place] = both.astype(jnp.bfloat16)
            k += 1


def combine(index, a, b):
    half = jax.ShapeDtypeStruct((8,) + a.shape[1:], jnp.bfloat16)
    return pl.pallas_call(
        add_blocks,
        in_specs=[pl.BlockSpec(memory_space=pltpu.SMEM)] + [pl.BlockSpec(memory_space=pltpu.VMEM)] * 2,
        out_specs=[pl.BlockSpec(memory_space=pltpu.VMEM)] * 2,
        out_shape=[half, half],
        compiler_params=pltpu.CompilerParams(vmem_limit_bytes=16 * 2**20),
        cost_estimate=pl.CostEstimate(flops=a.size, bytes_accessed=6 * a.size, transcendentals=0),
    )(jnp.stack(index), a, b)


def add_products(count, scale, *refs):
    out_ref = refs[-1]
    total_now = None
    for k in range(count):
        more = lax.dot_general(
            refs[k][...],
            refs[count + k][...],
            (((0,), (0,)), ((), ())),
            preferred_element_type=jnp.float32,
        )
        total_now = more if total_now is None else total_now + more
    if len(refs) > 2 * count + 1:
        total_now = total_now + refs[2 * count][...]
    out_ref[...] = (total_now * scale).astype(out_ref.dtype)


def weight_grad(pieces, rows, before, scale, dtype):
    columns, width = pieces[0].shape[1], rows[0].shape[1]
    wide = pl.BlockSpec((pieces[0].shape[0], 256), lambda i: (0, i))
    out = pl.BlockSpec((256, width), lambda i: (i, 0))
    return pl.pallas_call(
        functools.partial(add_products, len(pieces), scale),
        grid=(columns // 256,),
        in_specs=[wide] * len(pieces)
        + [pl.BlockSpec(rows[0].shape, lambda i: (0, 0))] * len(rows)
        + [out] * len(before),
        out_specs=out,
        out_shape=jax.ShapeDtypeStruct((columns, width), dtype),
        compiler_params=pltpu.CompilerParams(vmem_limit_bytes=24 * 2**20),
        cost_estimate=pl.CostEstimate(flops=0, bytes_accessed=0, transcendentals=0),
    )(*pieces, *rows, *before)


def places():
    zl, x, c, zh, y = (lax.axis_index(n) for n in ROW + COL)

    def orders(dc, dzl, dx):
        block = ((zl + dzl) % 2 * 4 + (x + dx) % 4) * 2 + (c + dc) % 2
        dy = (block % 4 - y) % 4
        return dy * 4 + block // 4, dy * 4 + (block // 4 - zh) % 4

    near = [orders(dc, dzl, dx) for dc in range(2) for dzl in range(2) for dx in range(4)]
    return [jnp.stack(v).astype(jnp.int32) for v in zip(*near)]


def keep_mark(mark_ref, out_ref):
    out_ref[...] = mark_ref[...]


def pass_mark(mark, flops):
    return pl.pallas_call(
        keep_mark,
        out_shape=jax.ShapeDtypeStruct(mark.shape, mark.dtype),
        cost_estimate=pl.CostEstimate(flops=flops, bytes_accessed=0, transcendentals=0),
    )(mark)


def drive(lanes, mark):
    asked, count = [next(lane) for lane in lanes], 0
    while lanes:
        sends = [send for more, _ in asked for send in more]
        inputs = [value for _, more in asked for value in more]
        held = fence(*[values for values, _, _ in sends], *inputs, mark)
        came = [shift(v, axis, step) for v, (_, axis, step) in zip(held, sends)]
        count += 1
        mark = pass_mark(held[-1], 0 if count in SHORT else ANCHOR)
        *held, mark = fence(*held[len(sends) : -1], mark)
        ends = []
        for lane, (more, values) in zip(lanes, asked):
            ends.append(lane.send((came[: len(more)], held[: len(values)])))
            came, held = came[len(more) :], held[len(values) :]
        *flat, mark = fence(*[value for end in ends for value in end], mark)
        going = []
        for lane, end in zip(lanes, ends):
            mine, flat = flat[: len(end)], flat[len(end) :]
            try:
                going.append((lane, lane.send(mine)))
            except StopIteration:
                pass
        lanes, asked = [lane for lane, _ in going], [ask for _, ask in going]


def idle(steps):
    for _ in range(steps):
        yield [], []
        yield []


def halves(values):
    cut = values.shape[1] // 2
    return values[:, :cut], values[:, cut:]


def total(*terms):
    return sum(t.astype(jnp.float32) for t in terms)


def with_half(values, half, side):
    parts = list(halves(values))
    parts[side] = total(parts[side], half).astype(jnp.bfloat16)
    return jnp.concatenate(parts, axis=1)


def post(sends, steps):
    came, _ = yield sends, []
    if steps > 1:
        yield []
        yield from idle(steps - 2)
        yield [], []
    return (yield came)


def post_swap(values, axis, steps):
    (came,) = yield from post([(values, axis, None)], steps)
    return came


def four(values):
    return jnp.stack([values] * 4)


def whole(pair):
    return jnp.concatenate(pair, axis=1)


def body(tokens, out_grad, pre_act, w_in, w_out):
    orders = places()
    bf16 = jnp.bfloat16
    f32 = jnp.float32
    grad_scale = float(2048) ** (-0.5)
    streams = (slice(0, WIDE), slice(WIDE, None))
    made = {}

    def row_gather(own, pause):
        (other,) = yield from post([(own, "zl", 1)], 1)
        yield from idle(pause)
        pair = jnp.stack([own, other])
        came = yield from post([(pair, "x", -1), (pair, "x", 2), (pair, "x", 1)], 1)
        chip = jnp.stack([pair] + came, axis=1).reshape(8, ROWS, 384)
        yield from idle(pause and 4)
        (far,) = yield from post([(chip, "c", 1)], 1)
        return reorder(orders, chip, far)

    def lane_grad():
        made["grad"] = yield from row_gather(out_grad, 0)

    def lane_tokens():
        made["tok"] = yield from row_gather(tokens, 3)

    def scatter_y(stream):
        grad, weight = made["grad"][0], w_out[streams[stream]]
        sends = []
        if stream == 0:
            for step, half in ((1, 0), (-1, 1)):
                rows = jnp.concatenate([jnp.split(w_out[s], 2)[half] for s in streams])
                sends.append((contract(grad[2], rows, 1, 1).astype(bf16), "y", step))
        came, rows = yield sends, [grad[1], grad[3]]
        came = yield came + [contract(r, weight, 1, 1).astype(bf16) for r in rows]
        if stream == 0:
            made["far"] = came[:2]
        else:
            _, came = yield [], list(made["far"]) + came
        up = with_half(came[2], halves(came[0])[stream], 0)
        down = with_half(came[3], halves(came[1])[stream], 1)
        if stream == 1:
            up, down = yield [up, down]
        came, rows = yield [(up, "y", 1), (down, "y", -1)], [grad[0]]
        came = yield came + [contract(rows[0], weight, 1, 1).astype(bf16)]
        return total(*came)

    def gather_y(stream, near):
        weight = w_in[:, streams[stream]]

        def part(piece):
            return contract(piece, weight, 1, 1).astype(bf16)

        came, held = yield [(near, "y", 1), (near, "y", -1)], [near]
        left, right, first = yield came + [part(held[0])]
        sends = [(halves(left)[0], "y", 1), (halves(right)[1], "y", -1)]
        came, held = yield sends, [right, left]
        *far, after, before = yield came + [part(h) for h in held]
        made["found", stream] = (near, right, whole(far), left)
        made["parts", stream] = jnp.stack([first, after, part(whole(far)), before]).reshape(16, ROWS, 384)

    def token_grads(stream, pieces, places_now):
        return sum(contract(made["tok"][stream][dy], p, 0, 0) for dy, p in zip(places_now, pieces))

    def lane_first():
        yield from idle(3)
        sums = (yield from scatter_y(0)).astype(bf16)
        came = yield from post_swap(sums.reshape(4, ROWS, -1), "zh", 2)
        pregrad = (jnp.sum(came.astype(f32), axis=0) * made["slopes"][:, streams[0]]).astype(bf16)
        near = (yield from post_swap(four(pregrad), "zh", 1)).reshape(4 * ROWS, -1)
        yield from gather_y(0, near)
        _, held = yield [], [*made["found", 0], made["parts", 0]]
        done = yield [token_grads(0, held[:4], range(4)), held[4]]
        made["w_in", 0], made["parts", 0] = done

    def lane_second():
        yield from idle(3)
        sums = (yield from scatter_y(1)).astype(bf16)
        here = lax.axis_index("zh")
        rows = [lax.dynamic_slice_in_dim(sums, (here + dz) % 4 * ROWS, ROWS, 0) for dz in range(4)]
        came = yield from post([(rows[dz], "zh", dz) for dz in (1, 2, 3)], 1)
        yield from idle(1)
        pregrad = (total(rows[0], *came) * made["slopes"][:, streams[1]]).astype(bf16)
        came = yield from post([(pregrad, "zh", -dz) for dz in (1, 2, 3)], 1)
        near = jnp.concatenate([pregrad] + came)
        yield from gather_y(1, near)

    def lane_act():
        _, held = yield [], [pre_act]
        activated, made["slopes"] = gelu_parts(held[0])
        copies, made["slopes"] = yield [four(activated.astype(bf16)), made["slopes"]]
        yield from idle(2)
        _, held = yield [], [copies]
        near = shift(held[0], "zh", None)
        yield []
        yield from idle(1)
        yield [], []
        (near,) = yield [near]
        near = near.reshape(4 * ROWS, -1)
        grad = made["grad"][0]
        came, _ = yield [(near, "y", 1), (near, "y", -1)], []
        yield []
        yield [], []
        left, right = yield came
        yield from idle(1)
        _, held = yield [], [near, right, left]
        rows = [grad[dy] for dy in (0, 1, 3)]
        ends = [halves(held[2])[0], halves(held[1])[1]]
        *ends, sums = yield ends + [weight_grad(held, rows, [], 1.0, f32)]
        yield from idle(1)
        far = yield from post([(ends[0], "y", 1), (ends[1], "y", -1)], 3)
        made["w_out"] = weight_grad([whole(far)], [grad[2]], [sums], grad_scale, bf16)

    def lane_row():
        yield from idle(11)
        keep, give = combine(orders, made["parts", 0], made["parts", 1])
        found = made["found", 1]
        came, held = yield [(give, "c", 1)], [found[0], found[1]]
        came, sums = yield came + [token_grads(1, held, (0, 1))]
        mine = total(keep, came).astype(bf16).reshape(2, 4, ROWS, 384)
        came, held = yield [(mine[:, dx], "x", dx) for dx in (1, 2, 3)], [found[2], found[3]]
        *came, sums = yield came + [sums + token_grads(1, held, (2, 3))]
        both = total(mine[:, 0], *came)
        came, held = yield [(both[1].astype(bf16), "zl", 1)], [made["w_in", 0], sums]
        came, made["w_in"] = yield came + [(whole(held) * grad_scale).astype(bf16)]
        made["tokens"] = total(both[0], came).astype(bf16)

    mark = pre_act[:8, :128].astype(f32)
    drive([lane_grad(), lane_tokens(), lane_act(), lane_first(), lane_second(), lane_row()], mark)
    return (made["tokens"], made["w_in"], made["w_out"])


def solution(mesh):
    fine = Mesh(mesh.devices.reshape(2, 4, 2, 4, 4), ROW + COL)
    in_specs = (P(ROW, COL), P(ROW, COL), P(COL, ROW), P(COL, ROW), P(ROW, COL))
    out_specs = (P(ROW, COL), P(COL, ROW), P(ROW, COL))
    return jax.shard_map(body, mesh=fine, in_specs=in_specs, out_specs=out_specs, check_vma=False)
```
